32 devices in a mesh: ch: 8 (over y, x, core), ta: 4 (over z).
Axes of the slice: x: 2, y: 2, z: 4, core: 2. Of those that a mesh axis runs over, the one named last changes fastest.
Arguments:
- raw: bfloat16 [2048, 20480], P('ch', 'ta'), may hold values from -40 to 40
- fir_taps: bfloat16 [129], replicated, may hold values from -0.5 to 0.5
- start_basis: float32 [512, 16], replicated, may hold values from -6 to 6
Outputs:
- cleaned: bfloat16 [2048, 20480], P('ch', 'ta')
The draws below stay inside these ranges and needn't reach their ends.
All inputs are finite; a program needn't handle non-finite values.
Results may differ from the reference program's by a relative error of at most 0.008.
Values may be sent and summed in bfloat16 or wider, within the bound.
A program may use at most 64 MiB of HBM per device.

```python
import math
import jax
import jax.numpy as jnp
from jax import lax

TAPS = 129
GAUGE = 4
STRIDE = 128
RANK = 16
ITERS = 6
WIN = 512
CHANNELS = 2048
TIME = 20480


def draw_raw(key, part):
    keys = jax.random.split(key, 4)
    noise = jnp.clip(jax.random.normal(keys[0], (CHANNELS, TIME), jnp.float32), -5.0, 5.0)
    scales = jnp.exp(jax.random.uniform(keys[1], (CHANNELS, 1), jnp.float32, jnp.log(0.3), jnp.log(3.0)))
    common = jnp.clip(jax.random.normal(keys[2], (1, TIME), jnp.float32), -4.0, 4.0)
    couple = 1.5 * jnp.clip(jax.random.normal(keys[3], (CHANNELS, 1), jnp.float32), -4.0, 4.0)
    values = scales * noise + couple * common
    return values.astype(jnp.bfloat16)


def scatter_about(stream_key, shape, scale, most, kind=jnp.bfloat16):
    result = jax.random.normal(stream_key, shape, jnp.float32) * scale
    return jnp.minimum(jnp.maximum(result, -most), most).astype(kind)


def setup_inputs(seed: int = 0) -> dict:
    key_list = jax.random.split(jax.random.key(seed), 4)
    raw = draw_raw(jax.random.fold_in(key_list[3], 71), 0)
    fir_taps = scatter_about(key_list[1], (TAPS,), TAPS ** -0.5, 0.5)
    start_basis = scatter_about(key_list[2], (WIN, RANK), 1.0, 6.0, jnp.float32)
    return {"raw": raw, "fir_taps": fir_taps, "start_basis": start_basis}


def toeplitz_band(taps, width):
    count = taps.shape[0]
    line = jnp.concatenate([taps, jnp.zeros((width,), taps.dtype)])
    flat = jnp.tile(line, width)[:width * (count + width - 1)]
    return flat.reshape(width, count + width - 1).T

def orthonormal(image):
    gram = jnp.dot(image.T, image, precision=lax.Precision.HIGHEST)
    lower = jnp.linalg.cholesky(gram)
    return lax.linalg.triangular_solve(lower, image, left_side=False, lower=True, transpose_a=True)

def reference(raw, fir_taps, start_basis):
    half = (TAPS - 1) // 2
    width = math.gcd(TIME, 512)
    padded = jnp.pad(raw, ((0, 0), (half, half)))
    band_matrix = toeplitz_band(fir_taps, width)

    def fir_block(number):
        piece = lax.dynamic_slice_in_dim(padded, number * width, width + TAPS - 1, 1)
        return jnp.dot(piece.astype(jnp.float32), band_matrix.astype(jnp.float32), preferred_element_type=jnp.float32)
    blocks = lax.map(fir_block, jnp.arange(TIME // width, dtype=jnp.int32))
    filtered = jnp.transpose(blocks, (1, 0, 2)).reshape(CHANNELS, TIME)
    rimmed = jnp.pad(filtered, ((GAUGE, GAUGE), (0, 0)))
    gauged = (rimmed[2 * GAUGE:] - rimmed[:-2 * GAUGE]).astype(jnp.bfloat16)
    framed = jnp.pad(gauged, ((2 * STRIDE, STRIDE), (0, 0)))

    def window(number):
        frame = lax.dynamic_slice_in_dim(framed, number * STRIDE, WIN, 0)
        scatter_mat = jnp.dot(frame.astype(jnp.float32), frame.T.astype(jnp.float32), preferred_element_type=jnp.float32) / TIME
        basis = start_basis
        for sweep in range(ITERS):
            basis = orthonormal(jnp.dot(scatter_mat, basis, precision=lax.Precision.HIGHEST))
        rounded = basis.astype(jnp.bfloat16)
        coeffs = jnp.dot(rounded.T.astype(jnp.float32), frame.astype(jnp.float32), preferred_element_type=jnp.float32).astype(jnp.bfloat16)
        fitted = jnp.dot(rounded[2 * STRIDE:3 * STRIDE].astype(jnp.float32), coeffs.astype(jnp.float32), preferred_element_type=jnp.float32)
        return (frame[2 * STRIDE:3 * STRIDE].astype(jnp.float32) - fitted).astype(jnp.bfloat16)
    cleaned = lax.map(window, jnp.arange(CHANNELS // STRIDE, dtype=jnp.int32))
    return cleaned.reshape(CHANNELS, TIME)
```

```python
import functools

import jax
import jax.numpy as jnp
from jax import lax
from jax.experimental import pallas as pl
from jax.experimental.pallas import tpu as pltpu
from jax.sharding import PartitionSpec as P

TAPS = 129
GAUGE = 4
STRIDE = 128
RANK = 16
ITERS = 6
WIN = 512
BLOCK = 256
EDGE = 128
MESH = pl.DeviceIdType.MESH

PLACE = {2: 0, 3: 128, 1: 256, 0: 384, 4: 512}


def toeplitz_band(taps, width):
    count = taps.shape[0]
    line = jnp.concatenate([taps, jnp.zeros((width,), taps.dtype)])
    flat = jnp.tile(line, width)[: width * (count + width - 1)]
    return flat.reshape(width, count + width - 1).T


def dot_nt(a, b):
    return lax.dot_general(a, b, (((1,), (1,)), ((), ())), preferred_element_type=jnp.float32)


def inverse_factor(gram):
    columns = [jnp.broadcast_to(gram[:, j : j + 1], (RANK, 128)) for j in range(RANK)]
    row = lax.broadcasted_iota(jnp.int32, (RANK, 128), 0)
    lane = lax.broadcasted_iota(jnp.int32, (RANK, 128), 1)
    inverse = jnp.where(row == lane, 1.0, 0.0).astype(jnp.float32)
    diagonal = jnp.ones((RANK, 128), jnp.float32)
    for k in range(RANK):
        column = columns[k]
        pivot = column[k : k + 1, :]
        diagonal = jnp.where(row == k, pivot, diagonal)
        if k == RANK - 1:
            break
        scaled = jnp.where(row > k, column * (1.0 / pivot), 0.0)
        for j in range(k + 1, RANK):
            columns[j] = columns[j] - scaled * column[j : j + 1, :]
        inverse = inverse - scaled * inverse[k : k + 1, :]
    inverse = inverse * lax.rsqrt(diagonal)
    return inverse[:, :RANK]


def split(value):
    high = value.astype(jnp.bfloat16)
    return high, (value - high.astype(jnp.float32)).astype(jnp.bfloat16)


def kernel(
    nch, nta, raw, band, start, out,
    x, gz, part, recv, s_hi, s_lo, basis,
    own_sem, halo_send, halo_recv, part_send, part_recv, basis_send, basis_recv,
):
    c = lax.axis_index("ch")
    t = lax.axis_index("ta")
    chans, samples = raw.shape
    right = EDGE + samples
    owners = (nta // 2 - 1, nta // 2)

    def exists(dc, dt):
        return (c + dc >= 0) & (c + dc < nch) & (t + dt >= 0) & (t + dt < nta)

    partners = [(dc, dt) for dc in (-2, -1, 0, 1, 2) for dt in (-1, 0, 1) if (dc, dt) != (0, 0)]
    partners += [(0, dt) for dt in range(1 - nta, nta) if abs(dt) > 1]

    own = pltpu.make_async_copy(raw, x.at[272:528, EDGE:right], own_sem)
    own.start()

    barrier = pltpu.get_barrier_semaphore()
    for dc, dt in partners:
        @pl.when(exists(dc, dt))
        def _():
            pl.semaphore_signal(barrier, inc=1, device_id=(c + dc, t + dt), device_id_type=MESH)
    near = 1 + sum(((c + dc >= 0) & (c + dc < nch)).astype(jnp.int32) for dc in (-2, -1, 1, 2))
    around = 1 + sum(((t + dt >= 0) & (t + dt < nta)).astype(jnp.int32) for dt in (-1, 1))
    pl.semaphore_wait(barrier, near * around - 1 + nta - around)

    mid = (EDGE, right)
    whole = (0, samples)
    low, high = (0, EDGE), (right, right + EDGE)
    head, tail = (0, EDGE), (samples - EDGE, samples)
    kinds = [
        (0, 1, (0, 256), tail, (272, 528), low),
        (0, -1, (0, 256), head, (272, 528), high),
        (1, 0, (240, 256), whole, (256, 272), mid),
        (-1, 0, (0, 16), whole, (528, 544), mid),
        (1, 1, (0, 256), tail, (16, 272), low),
        (1, -1, (0, 256), head, (16, 272), high),
        (-1, 1, (0, 144), tail, (528, 672), low),
        (-1, -1, (0, 144), head, (528, 672), high),
        (2, 0, (240, 256), whole, (0, 16), mid),
        (2, 1, (240, 256), tail, (0, 16), low),
        (2, -1, (240, 256), head, (0, 16), high),
        (1, 0, (112, 240), whole, (128, 256), mid),
        (-1, 0, (16, 144), whole, (544, 672), mid),
        (1, 0, (0, 112), whole, (16, 128), mid),
    ]

    def halo(index):
        dc, dt, rows, cols, to_rows, to_cols = kinds[index]
        return pltpu.make_async_remote_copy(
            src_ref=raw.at[rows[0] : rows[1], cols[0] : cols[1]],
            dst_ref=x.at[to_rows[0] : to_rows[1], to_cols[0] : to_cols[1]],
            send_sem=halo_send.at[index],
            recv_sem=halo_recv.at[index],
            device_id=(c + dc, t + dt),
            device_id_type=MESH,
        )

    def each_halo(indices, sign, act):
        for index in indices:
            dc, dt = kinds[index][:2]
            @pl.when(exists(sign * dc, sign * dt))
            def _():
                act(halo(index))

    everything = range(len(kinds))
    each_halo(everything, 1, lambda copy: copy.start())

    @pl.when(t == 0)
    def _():
        x[:, 0:EDGE] = jnp.zeros((x.shape[0], EDGE), x.dtype)

    @pl.when(t == nta - 1)
    def _():
        x[:, right : right + EDGE] = jnp.zeros((x.shape[0], EDGE), x.dtype)

    @pl.when(c == 0)
    def _():
        x[256:272, :] = jnp.zeros((16, x.shape[1]), x.dtype)

    @pl.when(c == 1)
    def _():
        x[0:16, :] = jnp.zeros((16, x.shape[1]), x.dtype)

    @pl.when(c == nch - 1)
    def _():
        x[528:544, :] = jnp.zeros((16, x.shape[1]), x.dtype)
        gz[512:640, :] = jnp.zeros((STRIDE, samples), gz.dtype)

    @pl.when(c == 0)
    def _():
        gz[256:512, :] = jnp.zeros((2 * STRIDE, samples), gz.dtype)

    def gauge(first, count):
        rows = STRIDE * count + 32
        @pl.loop(0, samples // BLOCK)
        def _(number):
            start_col = pl.multiple_of(number * BLOCK, BLOCK)
            piece = x[STRIDE * first : STRIDE * first + rows, pl.ds(start_col, 2 * BLOCK)]
            filtered = jnp.dot(piece, band[...], preferred_element_type=jnp.float32)
            for step in range(count):
                base = STRIDE * step
                upper = filtered[base + 20 : base + 20 + STRIDE]
                lower = filtered[base + 12 : base + 12 + STRIDE]
                place = PLACE[first + step]
                gz[place : place + STRIDE, pl.ds(start_col, BLOCK)] = (upper - lower).astype(gz.dtype)

    def products(groups):
        chunk = 1024
        for left, right_tile, place in groups:
            part[place : place + left[1] - left[0], :] = jnp.zeros((left[1] - left[0], STRIDE), jnp.float32)
        @pl.loop(0, samples // chunk)
        def _(number):
            cols = pl.ds(pl.multiple_of(number * chunk, chunk), chunk)
            for left, right_tile, place in groups:
                part[place : place + left[1] - left[0], :] += dot_nt(
                    gz[left[0] : left[1], cols], gz[right_tile : right_tile + STRIDE, cols]
                )

    spans = {
        ("own", 0): (0, 384, 0), ("own", 1): (0, 384, 0),
        ("next", 0): (384, 768, 384), ("next", 1): (384, 768, 384),
        ("far", 0): (1280, 1792, 768), ("far", 1): (768, 1280, 768),
    }
    order = {"own": 0, "next": 1, "far": 2}

    def part_copy(stage, window, source):
        begin, end, land = spans[stage, window]
        return pltpu.make_async_remote_copy(
            src_ref=part.at[begin:end],
            dst_ref=recv.at[source, land : land + end - begin],
            send_sem=part_send.at[window, order[stage]],
            recv_sem=part_recv.at[source, order[stage]],
            device_id=(c, owners[window]),
            device_id_type=MESH,
        )

    def send_part(stage, window):
        @pl.when(t != owners[window])
        def _():
            part_copy(stage, window, t).start()

    own.wait()
    each_halo(range(0, 8), -1, lambda copy: copy.wait_recv())
    gauge(2, 2)
    products([((0, 256), 0, 0), ((128, 256), 128, 256)])
    send_part("own", 0)
    send_part("own", 1)

    each_halo([11], -1, lambda copy: copy.wait_recv())
    @pl.when(c > 0)
    def _():
        gauge(1, 1)
    products([((0, 384), 256, 384)])
    send_part("next", 0)
    send_part("next", 1)

    each_halo([12], -1, lambda copy: copy.wait_recv())
    @pl.when(c < nch - 1)
    def _():
        gauge(4, 1)
    products([((0, 384), 512, 768), ((512, 640), 512, 1152)])
    send_part("far", 1)

    each_halo([8, 9, 10, 13], -1, lambda copy: copy.wait_recv())
    @pl.when(c > 0)
    def _():
        gauge(0, 1)
    products([((0, 512), 384, 1280)])
    send_part("far", 0)

    total_time = samples * nta

    def solve(window):
        for source in range(nta):
            if source != owners[window]:
                for stage in order:
                    part_copy(stage, window, source).wait_recv()

        blocks = {
            (0, 0): ("own", 0), (1, 0): ("own", 1), (1, 1): ("own", 2),
            (0, 2): ("next", 0), (1, 2): ("next", 1), (2, 2): ("next", 2),
            (0, 3): ("far", 0), (1, 3): ("far", 1), (2, 3): ("far", 2), (3, 3): ("far", 3),
        }
        for (p, q), (stage, number) in blocks.items():
            begin, _, land = spans[stage, window]
            begin, land = begin + STRIDE * number, land + STRIDE * number
            value = part[begin : begin + STRIDE, :]
            for source in range(nta):
                if source != owners[window]:
                    value = value + recv[source, land : land + STRIDE, :]
            value = value * (1.0 / total_time)
            for row, col, block in ((p, q, value), (q, p, value.T)):
                if (row, col) == (p, q) or p != q:
                    high_part, low_part = split(block)
                    where = (slice(STRIDE * row, STRIDE * (row + 1)), slice(STRIDE * col, STRIDE * (col + 1)))
                    s_hi[where] = high_part
                    s_lo[where] = low_part

        def sweep(_, current):
            high_part, low_part = split(current)
            both = jnp.concatenate([high_part, low_part], axis=0)
            image = jnp.dot(both, s_hi[...], preferred_element_type=jnp.float32)
            image = image[:RANK] + image[RANK:] + jnp.dot(
                high_part, s_lo[...], preferred_element_type=jnp.float32
            )
            gram = lax.dot_general(
                image, image, (((1,), (1,)), ((), ())),
                precision=lax.Precision.HIGHEST, preferred_element_type=jnp.float32,
            )
            return jnp.dot(
                inverse_factor(gram), image,
                precision=lax.Precision.HIGHEST, preferred_element_type=jnp.float32,
            )

        found = lax.fori_loop(0, ITERS, sweep, start[window]).astype(jnp.bfloat16)
        zero = jnp.zeros((RANK, STRIDE), jnp.bfloat16)
        last = [found[:, 384:512], zero] if window == 0 else [zero, found[:, 384:512]]
        basis[window] = jnp.concatenate([found[:, :384]] + last, axis=1)

    def basis_copy(window, target):
        return pltpu.make_async_remote_copy(
            src_ref=basis.at[window],
            dst_ref=basis.at[window],
            send_sem=basis_send.at[window, target],
            recv_sem=basis_recv.at[window],
            device_id=(c, target),
            device_id_type=MESH,
        )

    for window in (0, 1):
        @pl.when(t == owners[window])
        def _():
            solve(window)
            for target in range(nta):
                if target != owners[window]:
                    basis_copy(window, target).start()

    for window in (0, 1):
        @pl.when(t != owners[window])
        def _():
            basis_copy(window, owners[window]).wait_recv()

    both = jnp.concatenate([basis[0], basis[1]], axis=0)
    nothing = jnp.zeros((RANK, STRIDE), jnp.bfloat16)
    kept = jnp.concatenate(
        [
            jnp.concatenate([basis[0][:, 0:128], nothing], axis=1),
            jnp.concatenate([nothing, basis[1][:, 128:256]], axis=1),
        ],
        axis=0,
    )

    @pl.loop(0, samples // 512)
    def _(number):
        cols = pl.ds(pl.multiple_of(number * 512, 512), 512)
        coeffs = jnp.dot(both, gz[:, cols], preferred_element_type=jnp.float32).astype(jnp.bfloat16)
        fitted = lax.dot_general(
            kept, coeffs, (((0,), (0,)), ((), ())), preferred_element_type=jnp.float32
        )
        out[:, cols] = (gz[0:256, cols].astype(jnp.float32) - fitted).astype(out.dtype)

    each_halo(everything, 1, lambda copy: copy.wait_send())
    for window in (0, 1):
        @pl.when(t != owners[window])
        def _():
            for stage in order:
                part_copy(stage, window, t).wait_send()
        @pl.when(t == owners[window])
        def _():
            for target in range(nta):
                if target != owners[window]:
                    basis_copy(window, target).wait_send()


def per_device(nch, nta, raw, fir_taps, start_basis):
    chans, samples = raw.shape
    band = jnp.pad(toeplitz_band(fir_taps, BLOCK), ((64, 64), (0, 0)))
    tiles = start_basis.T.reshape(RANK, 4, STRIDE)
    start = jnp.stack([tiles[:, jnp.array(o), :].reshape(RANK, WIN) for o in ([2, 3, 1, 0], [1, 2, 0, 3])])
    vmem = pl.BlockSpec(memory_space=pltpu.VMEM)
    return pl.pallas_call(
        functools.partial(kernel, nch, nta),
        out_shape=jax.ShapeDtypeStruct((chans, samples), jnp.bfloat16),
        in_specs=[pl.BlockSpec(memory_space=pl.ANY), vmem, vmem],
        out_specs=vmem,
        scratch_shapes=[
            pltpu.VMEM((672, samples + 2 * EDGE), jnp.bfloat16),
            pltpu.VMEM((640, samples), jnp.bfloat16),
            pltpu.VMEM((14 * STRIDE, STRIDE), jnp.float32),
            pltpu.VMEM((nta, 10 * STRIDE, STRIDE), jnp.float32),
            pltpu.VMEM((WIN, WIN), jnp.bfloat16),
            pltpu.VMEM((WIN, WIN), jnp.bfloat16),
            pltpu.VMEM((2, RANK, 640), jnp.bfloat16),
            pltpu.SemaphoreType.DMA,
            pltpu.SemaphoreType.DMA((14,)),
            pltpu.SemaphoreType.DMA((14,)),
            pltpu.SemaphoreType.DMA((2, 3)),
            pltpu.SemaphoreType.DMA((nta, 3)),
            pltpu.SemaphoreType.DMA((2, nta)),
            pltpu.SemaphoreType.DMA((2,)),
        ],
        compiler_params=pltpu.CompilerParams(
            collective_id=0, has_side_effects=True, vmem_limit_bytes=48 * 1024 * 1024
        ),
    )(raw, band, start)


def solution(mesh):
    sizes = dict(mesh.shape)
    return jax.shard_map(
        functools.partial(per_device, sizes["ch"], sizes["ta"]),
        mesh=mesh,
        in_specs=(P("ch", "ta"), P(), P()),
        out_specs=P("ch", "ta"),
        check_vma=False,
    )
```

```python
import functools

import jax
import jax.numpy as jnp
from jax import lax
from jax.experimental import pallas as pl
from jax.experimental.pallas import tpu as pltpu
from jax.sharding import PartitionSpec as P

TAPS = 129
GAUGE = 4
STRIDE = 128
RANK = 16
ITERS = 6
WIN = 512
BLOCK = 256
EDGE = 128
MESH = pl.DeviceIdType.MESH

PLACE = {2: 0, 3: 128, 1: 256, 0: 384, 4: 512}


def dot_nt(a, b):
    return lax.dot_general(a, b, (((1,), (1,)), ((), ())), preferred_element_type=jnp.float32)


def inverse_factor(gram):
    columns = [jnp.broadcast_to(gram[:, j : j + 1], (RANK, 128)) for j in range(RANK)]
    row = lax.broadcasted_iota(jnp.int32, (RANK, 128), 0)
    lane = lax.broadcasted_iota(jnp.int32, (RANK, 128), 1)
    inverse = jnp.where(row == lane % RANK, 1.0, 0.0).astype(jnp.float32)
    diagonal = jnp.ones((RANK, 128), jnp.float32)
    for k in range(RANK):
        column = columns[k]
        pivot = column[k : k + 1, :]
        diagonal = jnp.where(row == k, pivot, diagonal)
        if k == RANK - 1:
            break
        scaled = jnp.where(row > k, column * (1.0 / pivot), 0.0)
        for j in range(k + 1, RANK):
            columns[j] = columns[j] - scaled * column[j : j + 1, :]
        inverse = inverse - scaled * inverse[k : k + 1, :]
    return inverse * lax.rsqrt(diagonal)


def split(value):
    high = value.astype(jnp.bfloat16)
    return high, (value - high.astype(jnp.float32)).astype(jnp.bfloat16)


def split_three(value):
    high = value.astype(jnp.bfloat16)
    rest = value - high.astype(jnp.float32)
    middle = rest.astype(jnp.bfloat16)
    return high, middle, (rest - middle.astype(jnp.float32)).astype(jnp.bfloat16)


def gram_of(parts):
    stacked = jnp.concatenate(parts, axis=0)
    terms = dot_nt(stacked, stacked)
    rows = terms[:RANK] + (terms[RANK : 2 * RANK] + terms[2 * RANK :])
    return rows[:, :RANK] + (rows[:, RANK : 2 * RANK] + rows[:, 2 * RANK :])


def apply_inverse(inverse, parts):
    lane = lax.broadcasted_iota(jnp.int32, inverse.shape, 1)
    high, middle, low = (part.astype(jnp.float32) for part in split_three(inverse))
    left = jnp.where(lane < 3 * RANK, high, jnp.where(lane < 5 * RANK, middle, low))
    left = jnp.where(lane < 6 * RANK, left, 0.0).astype(jnp.bfloat16)
    zero = jnp.zeros((2 * RANK, WIN), jnp.bfloat16)
    right = jnp.concatenate(
        [parts[0], parts[1], parts[2], parts[0], parts[1], parts[0], zero], axis=0
    )
    return jnp.dot(left, right, preferred_element_type=jnp.float32)


def kernel(
    nch, nta, raw, taps, start, out,
    x, gz, band, part, recv, s_hi, s_lo, basis,
    own_sem, halo_send, halo_recv, part_send, part_recv, basis_send, basis_recv,
):
    c = lax.axis_index("ch")
    t = lax.axis_index("ta")
    chans, samples = raw.shape
    right = EDGE + samples
    owners = (nta // 2 - 1, nta // 2)

    def exists(dc, dt):
        return (c + dc >= 0) & (c + dc < nch) & (t + dt >= 0) & (t + dt < nta)

    partners = [(dc, dt) for dc in (-2, -1, 0, 1, 2) for dt in (-1, 0, 1) if (dc, dt) != (0, 0)]
    partners += [(0, dt) for dt in range(1 - nta, nta) if abs(dt) > 1]

    own = pltpu.make_async_copy(raw, x.at[272:528, EDGE:right], own_sem)
    own.start()

    barrier = pltpu.get_barrier_semaphore()
    for dc, dt in partners:
        @pl.when(exists(dc, dt))
        def _():
            pl.semaphore_signal(barrier, inc=1, device_id=(c + dc, t + dt), device_id_type=MESH)
    near = 1 + sum(((c + dc >= 0) & (c + dc < nch)).astype(jnp.int32) for dc in (-2, -1, 1, 2))
    around = 1 + sum(((t + dt >= 0) & (t + dt < nta)).astype(jnp.int32) for dt in (-1, 1))
    pl.semaphore_wait(barrier, near * around - 1 + nta - around)

    mid = (EDGE, right)
    whole = (0, samples)
    low, high = (0, EDGE), (right, right + EDGE)
    head, tail = (0, EDGE), (samples - EDGE, samples)
    kinds = [
        (0, 1, (0, 256), tail, (272, 528), low),
        (0, -1, (0, 256), head, (272, 528), high),
        (1, 0, (240, 256), whole, (256, 272), mid),
        (-1, 0, (0, 16), whole, (528, 544), mid),
        (1, 1, (0, 256), tail, (16, 272), low),
        (1, -1, (0, 256), head, (16, 272), high),
        (-1, 1, (0, 144), tail, (528, 672), low),
        (-1, -1, (0, 144), head, (528, 672), high),
        (2, 0, (240, 256), whole, (0, 16), mid),
        (2, 1, (240, 256), tail, (0, 16), low),
        (2, -1, (240, 256), head, (0, 16), high),
        (1, 0, (112, 240), whole, (128, 256), mid),
        (-1, 0, (16, 144), whole, (544, 672), mid),
        (1, 0, (0, 112), whole, (16, 128), mid),
    ]

    def halo(index):
        dc, dt, rows, cols, to_rows, to_cols = kinds[index]
        return pltpu.make_async_remote_copy(
            src_ref=raw.at[rows[0] : rows[1], cols[0] : cols[1]],
            dst_ref=x.at[to_rows[0] : to_rows[1], to_cols[0] : to_cols[1]],
            send_sem=halo_send.at[index],
            recv_sem=halo_recv.at[index],
            device_id=(c + dc, t + dt),
            device_id_type=MESH,
        )

    def each_halo(indices, sign, act):
        for index in indices:
            dc, dt = kinds[index][:2]
            @pl.when(exists(sign * dc, sign * dt))
            def _():
                act(halo(index))

    everything = range(len(kinds))
    each_halo(everything, 1, lambda copy: copy.start())

    lines = jnp.broadcast_to(taps[...], (BLOCK, 2 * BLOCK))
    lines = pltpu.roll(lines, 64, 1, stride=1, stride_axis=0)
    band[...] = lines.T.astype(band.dtype)

    @pl.when(t == 0)
    def _():
        x[:, 0:EDGE] = jnp.zeros((x.shape[0], EDGE), x.dtype)

    @pl.when(t == nta - 1)
    def _():
        x[:, right : right + EDGE] = jnp.zeros((x.shape[0], EDGE), x.dtype)

    @pl.when(c == 0)
    def _():
        x[256:272, :] = jnp.zeros((16, x.shape[1]), x.dtype)

    @pl.when(c == 1)
    def _():
        x[0:16, :] = jnp.zeros((16, x.shape[1]), x.dtype)

    @pl.when(c == nch - 1)
    def _():
        x[528:544, :] = jnp.zeros((16, x.shape[1]), x.dtype)
        gz[512:640, :] = jnp.zeros((STRIDE, samples), gz.dtype)

    @pl.when(c == 0)
    def _():
        gz[256:512, :] = jnp.zeros((2 * STRIDE, samples), gz.dtype)

    def gauge(first, count):
        rows = STRIDE * count + 32
        @pl.loop(0, samples // BLOCK)
        def _(number):
            start_col = pl.multiple_of(number * BLOCK, BLOCK)
            piece = x[STRIDE * first : STRIDE * first + rows, pl.ds(start_col, 2 * BLOCK)]
            filtered = jnp.dot(piece, band[...], preferred_element_type=jnp.float32)
            for step in range(count):
                base = STRIDE * step
                upper = filtered[base + 20 : base + 20 + STRIDE]
                lower = filtered[base + 12 : base + 12 + STRIDE]
                place = PLACE[first + step]
                gz[place : place + STRIDE, pl.ds(start_col, BLOCK)] = (upper - lower).astype(gz.dtype)

    def products(groups):
        chunk = 1024
        for left, right_tile, place in groups:
            part[place : place + left[1] - left[0], :] = jnp.zeros((left[1] - left[0], STRIDE), jnp.float32)
        @pl.loop(0, samples // chunk)
        def _(number):
            cols = pl.ds(pl.multiple_of(number * chunk, chunk), chunk)
            for left, right_tile, place in groups:
                part[place : place + left[1] - left[0], :] += dot_nt(
                    gz[left[0] : left[1], cols], gz[right_tile : right_tile + STRIDE, cols]
                )

    spans = {
        ("own", 0): (0, 384, 0), ("own", 1): (0, 384, 0),
        ("next", 0): (384, 768, 384), ("next", 1): (384, 768, 384),
        ("far", 0): (1280, 1792, 768), ("far", 1): (768, 1280, 768),
    }
    order = {"own": 0, "next": 1, "far": 2}

    def part_copy(stage, window, source):
        begin, end, land = spans[stage, window]
        return pltpu.make_async_remote_copy(
            src_ref=part.at[begin:end],
            dst_ref=recv.at[source, land : land + end - begin],
            send_sem=part_send.at[window, order[stage]],
            recv_sem=part_recv.at[source, order[stage]],
            device_id=(c, owners[window]),
            device_id_type=MESH,
        )

    def send_part(stage, window):
        @pl.when(t != owners[window])
        def _():
            part_copy(stage, window, t).start()

    own.wait()
    each_halo(range(0, 8), -1, lambda copy: copy.wait_recv())
    gauge(2, 2)
    products([((0, 256), 0, 0), ((128, 256), 128, 256)])
    send_part("own", 0)
    send_part("own", 1)

    each_halo([11], -1, lambda copy: copy.wait_recv())
    @pl.when(c > 0)
    def _():
        gauge(1, 1)
    products([((0, 384), 256, 384)])
    send_part("next", 0)
    send_part("next", 1)

    def tile_after():
        each_halo([12], -1, lambda copy: copy.wait_recv())
        @pl.when(c < nch - 1)
        def _():
            gauge(4, 1)
        products([((0, 384), 512, 768), ((512, 640), 512, 1152)])
        send_part("far", 1)

    def first_tile():
        each_halo([8, 9, 10, 13], -1, lambda copy: copy.wait_recv())
        @pl.when(c > 0)
        def _():
            gauge(0, 1)
        products([((0, 512), 384, 1280)])
        send_part("far", 0)

    @pl.when(c % 2 == 1)
    def _():
        first_tile()
    tile_after()
    @pl.when(c % 2 == 0)
    def _():
        first_tile()

    total_time = samples * nta

    def solve(window):
        for source in range(nta):
            if source != owners[window]:
                for stage in order:
                    part_copy(stage, window, source).wait_recv()

        blocks = {
            (0, 0): ("own", 0), (1, 0): ("own", 1), (1, 1): ("own", 2),
            (0, 2): ("next", 0), (1, 2): ("next", 1), (2, 2): ("next", 2),
            (0, 3): ("far", 0), (1, 3): ("far", 1), (2, 3): ("far", 2), (3, 3): ("far", 3),
        }
        for (p, q), (stage, number) in blocks.items():
            begin, _, land = spans[stage, window]
            begin, land = begin + STRIDE * number, land + STRIDE * number
            value = part[begin : begin + STRIDE, :]
            for source in range(nta):
                if source != owners[window]:
                    value = value + recv[source, land : land + STRIDE, :]
            value = value * (1.0 / total_time)
            for row, col, block in ((p, q, value), (q, p, value.T)):
                if (row, col) == (p, q) or p != q:
                    high_part, low_part = split(block)
                    where = (slice(STRIDE * row, STRIDE * (row + 1)), slice(STRIDE * col, STRIDE * (col + 1)))
                    s_hi[where] = high_part
                    s_lo[where] = low_part

        def sweep(_, current):
            high_part, low_part = split(current)
            both = jnp.concatenate([high_part, low_part], axis=0)
            image = jnp.dot(both, s_hi[...], preferred_element_type=jnp.float32)
            image = image[:RANK] + image[RANK:] + jnp.dot(
                high_part, s_lo[...], preferred_element_type=jnp.float32
            )
            parts = split_three(image)
            return apply_inverse(inverse_factor(gram_of(parts)), parts)

        places = (2, 3, 1, 0) if window == 0 else (1, 2, 0, 3)
        first = jnp.concatenate([start[:, STRIDE * p : STRIDE * (p + 1)] for p in places], axis=1)
        found = lax.fori_loop(0, ITERS, sweep, first).astype(jnp.bfloat16)
        zero = jnp.zeros((RANK, STRIDE), jnp.bfloat16)
        last = [found[:, 384:512], zero] if window == 0 else [zero, found[:, 384:512]]
        basis[window] = jnp.concatenate([found[:, :384]] + last, axis=1)

    def basis_copy(window, target):
        return pltpu.make_async_remote_copy(
            src_ref=basis.at[window],
            dst_ref=basis.at[window],
            send_sem=basis_send.at[window, target],
            recv_sem=basis_recv.at[window],
            device_id=(c, target),
            device_id_type=MESH,
        )

    for window in (0, 1):
        @pl.when(t == owners[window])
        def _():
            solve(window)
            for target in range(nta):
                if target != owners[window]:
                    basis_copy(window, target).start()

    for window in (0, 1):
        @pl.when(t != owners[window])
        def _():
            basis_copy(window, owners[window]).wait_recv()

    both = jnp.concatenate([basis[0], basis[1]], axis=0)
    nothing = jnp.zeros((RANK, STRIDE), jnp.bfloat16)
    kept = jnp.concatenate(
        [
            jnp.concatenate([basis[0][:, 0:128], nothing], axis=1),
            jnp.concatenate([nothing, basis[1][:, 128:256]], axis=1),
        ],
        axis=0,
    )

    @pl.loop(0, samples // 512)
    def _(number):
        cols = pl.ds(pl.multiple_of(number * 512, 512), 512)
        coeffs = jnp.dot(both, gz[:, cols], preferred_element_type=jnp.float32).astype(jnp.bfloat16)
        fitted = lax.dot_general(
            kept, coeffs, (((0,), (0,)), ((), ())), preferred_element_type=jnp.float32
        )
        out[:, cols] = (gz[0:256, cols].astype(jnp.float32) - fitted).astype(out.dtype)

    each_halo(everything, 1, lambda copy: copy.wait_send())
    for window in (0, 1):
        @pl.when(t != owners[window])
        def _():
            for stage in order:
                part_copy(stage, window, t).wait_send()
        @pl.when(t == owners[window])
        def _():
            for target in range(nta):
                if target != owners[window]:
                    basis_copy(window, target).wait_send()


def per_device(nch, nta, raw, fir_taps, start_basis):
    chans, samples = raw.shape
    taps = jnp.pad(fir_taps.astype(jnp.float32), (0, 2 * BLOCK - TAPS))[None]
    vmem = pl.BlockSpec(memory_space=pltpu.VMEM)
    return pl.pallas_call(
        functools.partial(kernel, nch, nta),
        out_shape=jax.ShapeDtypeStruct((chans, samples), jnp.bfloat16),
        in_specs=[pl.BlockSpec(memory_space=pl.ANY), vmem, vmem],
        out_specs=vmem,
        scratch_shapes=[
            pltpu.VMEM((672, samples + 2 * EDGE), jnp.bfloat16),
            pltpu.VMEM((640, samples), jnp.bfloat16),
            pltpu.VMEM((2 * BLOCK, BLOCK), jnp.bfloat16),
            pltpu.VMEM((14 * STRIDE, STRIDE), jnp.float32),
            pltpu.VMEM((nta, 10 * STRIDE, STRIDE), jnp.float32),
            pltpu.VMEM((WIN, WIN), jnp.bfloat16),
            pltpu.VMEM((WIN, WIN), jnp.bfloat16),
            pltpu.VMEM((2, RANK, 640), jnp.bfloat16),
            pltpu.SemaphoreType.DMA,
            pltpu.SemaphoreType.DMA((14,)),
            pltpu.SemaphoreType.DMA((14,)),
            pltpu.SemaphoreType.DMA((2, 3)),
            pltpu.SemaphoreType.DMA((nta, 3)),
            pltpu.SemaphoreType.DMA((2, nta)),
            pltpu.SemaphoreType.DMA((2,)),
        ],
        compiler_params=pltpu.CompilerParams(
            collective_id=0, has_side_effects=True, vmem_limit_bytes=48 * 1024 * 1024
        ),
    )(raw, taps, start_basis.T)


def solution(mesh):
    sizes = dict(mesh.shape)
    return jax.shard_map(
        functools.partial(per_device, sizes["ch"], sizes["ta"]),
        mesh=mesh,
        in_specs=(P("ch", "ta"), P(), P()),
        out_specs=P("ch", "ta"),
        check_vma=False,
    )
```

```python
import functools
import math

import jax
import jax.numpy as jnp
from jax import lax
from jax.experimental import pallas as pl
from jax.experimental.pallas import tpu as pltpu
from jax.sharding import PartitionSpec as P

TAPS = 129
GAUGE = 4
STRIDE = 128
RANK = 16
ITERS = 6
WIN = 512
BLOCK = 256
EDGE = 128
MESH = pl.DeviceIdType.MESH

PLACE = {2: 0, 3: 128, 1: 256, 0: 384, 4: 512}


def dot_nt(a, b):
    return lax.dot_general(a, b, (((1,), (1,)), ((), ())), preferred_element_type=jnp.float32)


def inverse_factor(gram):
    columns = [jnp.broadcast_to(gram[:, j : j + 1], (RANK, 128)) for j in range(RANK)]
    row = lax.broadcasted_iota(jnp.int32, (RANK, 128), 0)
    lane = lax.broadcasted_iota(jnp.int32, (RANK, 128), 1)
    inverse = jnp.where(row == lane % RANK, 1.0, 0.0).astype(jnp.float32)
    diagonal = jnp.ones((RANK, 128), jnp.float32)

    def spread(value, index):
        return jnp.broadcast_to(value[index : index + 1, :], (RANK, 128))

    for first in range(0, RANK, 4):
        block = range(first, first + 4)
        lead = {(i, j): spread(columns[j], i) for j in block for i in block if i >= j}
        lines = {k: spread(inverse, k) for k in block}
        scaled = {}
        for k in block:
            pivot = lead[k, k]
            diagonal = jnp.where(row == k, pivot, diagonal)
            reciprocal = 1.0 / pivot
            scaled[k] = jnp.where(row > k, columns[k] * reciprocal, 0.0)
            for j in range(k + 1, first + 4):
                ratio = lead[j, k] * reciprocal
                for i in range(j, first + 4):
                    lead[i, j] = lead[i, j] - ratio * lead[i, k]
                columns[j] = columns[j] - scaled[k] * lead[j, k]
                lines[j] = lines[j] - ratio * lines[k]
        for j in range(first + 4, RANK):
            for k in block:
                columns[j] = columns[j] - scaled[k] * spread(columns[k], j)
        for k in block:
            inverse = inverse - scaled[k] * lines[k]
    return inverse * lax.rsqrt(diagonal)


def split(value):
    high = value.astype(jnp.bfloat16)
    return high, (value - high.astype(jnp.float32)).astype(jnp.bfloat16)


def split_three(value):
    high = value.astype(jnp.bfloat16)
    rest = value - high.astype(jnp.float32)
    middle = rest.astype(jnp.bfloat16)
    return high, middle, (rest - middle.astype(jnp.float32)).astype(jnp.bfloat16)


def gram_of(parts):
    stacked = jnp.concatenate(parts, axis=0)
    terms = dot_nt(stacked, stacked)
    rows = terms[:RANK] + (terms[RANK : 2 * RANK] + terms[2 * RANK :])
    return rows[:, :RANK] + (rows[:, RANK : 2 * RANK] + rows[:, 2 * RANK :])


def apply_inverse(inverse, parts):
    lane = lax.broadcasted_iota(jnp.int32, inverse.shape, 1)
    high, middle, low = (part.astype(jnp.float32) for part in split_three(inverse))
    left = jnp.where(lane < 3 * RANK, high, jnp.where(lane < 5 * RANK, middle, low))
    left = jnp.where(lane < 6 * RANK, left, 0.0).astype(jnp.bfloat16)
    zero = jnp.zeros((2 * RANK, WIN), jnp.bfloat16)
    right = jnp.concatenate(
        [parts[0], parts[1], parts[2], parts[0], parts[1], parts[0], zero], axis=0
    )
    return jnp.dot(left, right, preferred_element_type=jnp.float32)


def kernel(
    nch, nta, raw, taps_in, start_in, out,
    taps, start, small_sem, x, gz, band, part, recv, s_hi, s_lo, basis,
    own_sem, halo_send, halo_recv, part_send, part_recv, basis_send, basis_recv,
):
    c = lax.axis_index("ch")
    t = lax.axis_index("ta")
    chans, samples = raw.shape
    right = EDGE + samples
    owners = (nta // 2 - 1, nta // 2)

    def exists(dc, dt):
        return (c + dc >= 0) & (c + dc < nch) & (t + dt >= 0) & (t + dt < nta)

    partners = [(dc, dt) for dc in (-2, -1, 0, 1, 2) for dt in (-1, 0, 1) if (dc, dt) != (0, 0)]
    partners += [(0, dt) for dt in range(1 - nta, nta) if abs(dt) > 1]

    own = pltpu.make_async_copy(raw, x.at[272:528, EDGE:right], own_sem)
    own.start()
    taps_copy = pltpu.make_async_copy(taps_in, taps, small_sem.at[0])
    start_copy = pltpu.make_async_copy(start_in, start, small_sem.at[1])
    taps_copy.start()
    start_copy.start()

    barrier = pltpu.get_barrier_semaphore()
    for dc, dt in partners:
        @pl.when(exists(dc, dt))
        def _():
            pl.semaphore_signal(barrier, inc=1, device_id=(c + dc, t + dt), device_id_type=MESH)
    near = 1 + sum(((c + dc >= 0) & (c + dc < nch)).astype(jnp.int32) for dc in (-2, -1, 1, 2))
    around = 1 + sum(((t + dt >= 0) & (t + dt < nta)).astype(jnp.int32) for dt in (-1, 1))
    pl.semaphore_wait(barrier, near * around - 1 + nta - around)

    mid = (EDGE, right)
    whole = (0, samples)
    low, high = (0, EDGE), (right, right + EDGE)
    head, tail = (0, EDGE), (samples - EDGE, samples)
    kinds = [
        (0, 1, (0, 256), tail, (272, 528), low),
        (0, -1, (0, 256), head, (272, 528), high),
        (1, 0, (240, 256), whole, (256, 272), mid),
        (-1, 0, (0, 16), whole, (528, 544), mid),
        (1, 1, (0, 256), tail, (16, 272), low),
        (1, -1, (0, 256), head, (16, 272), high),
        (-1, 1, (0, 144), tail, (528, 672), low),
        (-1, -1, (0, 144), head, (528, 672), high),
        (2, 0, (240, 256), whole, (0, 16), mid),
        (2, 1, (240, 256), tail, (0, 16), low),
        (2, -1, (240, 256), head, (0, 16), high),
        (1, 0, (112, 240), whole, (128, 256), mid),
        (-1, 0, (16, 144), whole, (544, 672), mid),
        (1, 0, (0, 112), whole, (16, 128), mid),
    ]

    def halo(index):
        dc, dt, rows, cols, to_rows, to_cols = kinds[index]
        return pltpu.make_async_remote_copy(
            src_ref=raw.at[rows[0] : rows[1], cols[0] : cols[1]],
            dst_ref=x.at[to_rows[0] : to_rows[1], to_cols[0] : to_cols[1]],
            send_sem=halo_send.at[index],
            recv_sem=halo_recv.at[index],
            device_id=(c + dc, t + dt),
            device_id_type=MESH,
        )

    def each_halo(indices, sign, act):
        for index in indices:
            dc, dt = kinds[index][:2]
            @pl.when(exists(sign * dc, sign * dt))
            def _():
                act(halo(index))

    everything = range(len(kinds))
    each_halo(everything, 1, lambda copy: copy.start())

    taps_copy.wait()
    start_copy.wait()
    lines = jnp.broadcast_to(taps[...], (BLOCK, 2 * BLOCK))
    lines = pltpu.roll(lines, 64, 1, stride=1, stride_axis=0)
    band[...] = lines.T.astype(band.dtype)

    @pl.when(t == 0)
    def _():
        x[:, 0:EDGE] = jnp.zeros((x.shape[0], EDGE), x.dtype)

    @pl.when(t == nta - 1)
    def _():
        x[:, right : right + EDGE] = jnp.zeros((x.shape[0], EDGE), x.dtype)

    @pl.when(c == 0)
    def _():
        x[256:272, :] = jnp.zeros((16, x.shape[1]), x.dtype)

    @pl.when(c == 1)
    def _():
        x[0:16, :] = jnp.zeros((16, x.shape[1]), x.dtype)

    @pl.when(c == nch - 1)
    def _():
        x[528:544, :] = jnp.zeros((16, x.shape[1]), x.dtype)
        gz[512:640, :] = jnp.zeros((STRIDE, samples), gz.dtype)

    @pl.when(c == 0)
    def _():
        gz[256:512, :] = jnp.zeros((2 * STRIDE, samples), gz.dtype)

    def gauge(first, count):
        rows = STRIDE * count + 32
        together = math.gcd(samples // BLOCK, 5)
        @pl.loop(0, samples // (BLOCK * together))
        def _(number):
            start_col = pl.multiple_of(number * (BLOCK * together), BLOCK)
            pieces = [
                x[STRIDE * first : STRIDE * first + rows, pl.ds(start_col + BLOCK * p, 2 * BLOCK)]
                for p in range(together)
            ]
            filtered = jnp.dot(
                jnp.concatenate(pieces, axis=0), band[...], preferred_element_type=jnp.float32
            )
            for p in range(together):
                for step in range(count):
                    base = rows * p + STRIDE * step
                    upper = filtered[base + 20 : base + 20 + STRIDE]
                    lower = filtered[base + 12 : base + 12 + STRIDE]
                    place = PLACE[first + step]
                    gz[place : place + STRIDE, pl.ds(start_col + BLOCK * p, BLOCK)] = (
                        upper - lower
                    ).astype(gz.dtype)

    def products(groups):
        chunk = 1024
        for left, right_tile, place in groups:
            part[place : place + left[1] - left[0], :] = jnp.zeros((left[1] - left[0], STRIDE), jnp.float32)
        @pl.loop(0, samples // chunk)
        def _(number):
            cols = pl.ds(pl.multiple_of(number * chunk, chunk), chunk)
            for left, right_tile, place in groups:
                part[place : place + left[1] - left[0], :] += dot_nt(
                    gz[left[0] : left[1], cols], gz[right_tile : right_tile + STRIDE, cols]
                )

    spans = {
        ("own", 0): (0, 384, 0), ("own", 1): (0, 384, 0),
        ("next", 0): (384, 768, 384), ("next", 1): (384, 768, 384),
        ("far", 0): (1280, 1792, 768), ("far", 1): (768, 1280, 768),
    }
    order = {"own": 0, "next": 1, "far": 2}

    def part_copy(stage, window, source):
        begin, end, land = spans[stage, window]
        return pltpu.make_async_remote_copy(
            src_ref=part.at[begin:end],
            dst_ref=recv.at[source, land : land + end - begin],
            send_sem=part_send.at[window, order[stage]],
            recv_sem=part_recv.at[source, order[stage]],
            device_id=(c, owners[window]),
            device_id_type=MESH,
        )

    def send_part(stage, window):
        @pl.when(t != owners[window])
        def _():
            part_copy(stage, window, t).start()

    own.wait()
    each_halo(range(0, 8), -1, lambda copy: copy.wait_recv())
    gauge(2, 2)
    products([((0, 256), 0, 0), ((128, 256), 128, 256)])
    send_part("own", 0)
    send_part("own", 1)

    each_halo([11], -1, lambda copy: copy.wait_recv())
    @pl.when(c > 0)
    def _():
        gauge(1, 1)
    products([((0, 384), 256, 384)])
    send_part("next", 0)
    send_part("next", 1)

    def tile_after():
        each_halo([12], -1, lambda copy: copy.wait_recv())
        @pl.when(c < nch - 1)
        def _():
            gauge(4, 1)
        products([((0, 384), 512, 768), ((512, 640), 512, 1152)])
        send_part("far", 1)

    def first_tile():
        each_halo([8, 9, 10, 13], -1, lambda copy: copy.wait_recv())
        @pl.when(c > 0)
        def _():
            gauge(0, 1)
        products([((0, 512), 384, 1280)])
        send_part("far", 0)

    @pl.when(c % 2 == 1)
    def _():
        first_tile()
    tile_after()
    @pl.when(c % 2 == 0)
    def _():
        first_tile()

    total_time = samples * nta

    def solve(window):
        for source in range(nta):
            if source != owners[window]:
                for stage in order:
                    part_copy(stage, window, source).wait_recv()

        blocks = {
            (0, 0): ("own", 0), (1, 0): ("own", 1), (1, 1): ("own", 2),
            (0, 2): ("next", 0), (1, 2): ("next", 1), (2, 2): ("next", 2),
            (0, 3): ("far", 0), (1, 3): ("far", 1), (2, 3): ("far", 2), (3, 3): ("far", 3),
        }
        for (p, q), (stage, number) in blocks.items():
            begin, _, land = spans[stage, window]
            begin, land = begin + STRIDE * number, land + STRIDE * number
            value = part[begin : begin + STRIDE, :]
            for source in range(nta):
                if source != owners[window]:
                    value = value + recv[source, land : land + STRIDE, :]
            value = value * (1.0 / total_time)
            for row, col, block in ((p, q, value), (q, p, value.T)):
                if (row, col) == (p, q) or p != q:
                    high_part, low_part = split(block)
                    where = (slice(STRIDE * row, STRIDE * (row + 1)), slice(STRIDE * col, STRIDE * (col + 1)))
                    s_hi[where] = high_part
                    s_lo[where] = low_part

        def sweep(_, current):
            high_part, low_part = split(current)
            both = jnp.concatenate([high_part, low_part], axis=0)
            image = jnp.dot(both, s_hi[...], preferred_element_type=jnp.float32)
            image = image[:RANK] + image[RANK:] + jnp.dot(
                high_part, s_lo[...], preferred_element_type=jnp.float32
            )
            parts = split_three(image)
            return apply_inverse(inverse_factor(gram_of(parts)), parts)

        places = (2, 3, 1, 0) if window == 0 else (1, 2, 0, 3)
        first = jnp.concatenate([start[:, STRIDE * p : STRIDE * (p + 1)] for p in places], axis=1)
        found = lax.fori_loop(0, ITERS, sweep, first).astype(jnp.bfloat16)
        zero = jnp.zeros((RANK, STRIDE), jnp.bfloat16)
        last = [found[:, 384:512], zero] if window == 0 else [zero, found[:, 384:512]]
        basis[window] = jnp.concatenate([found[:, :384]] + last, axis=1)

    def basis_copy(window, target):
        return pltpu.make_async_remote_copy(
            src_ref=basis.at[window],
            dst_ref=basis.at[window],
            send_sem=basis_send.at[window, target],
            recv_sem=basis_recv.at[window],
            device_id=(c, target),
            device_id_type=MESH,
        )

    for window in (0, 1):
        @pl.when(t == owners[window])
        def _():
            solve(window)
            for target in range(nta):
                if target != owners[window]:
                    basis_copy(window, target).start()

    for window in (0, 1):
        @pl.when(t != owners[window])
        def _():
            basis_copy(window, owners[window]).wait_recv()

    both = jnp.concatenate([basis[0], basis[1]], axis=0)
    nothing = jnp.zeros((RANK, STRIDE), jnp.bfloat16)
    kept = jnp.concatenate(
        [
            jnp.concatenate([basis[0][:, 0:128], nothing], axis=1),
            jnp.concatenate([nothing, basis[1][:, 128:256]], axis=1),
        ],
        axis=0,
    )

    @pl.loop(0, samples // 512)
    def _(number):
        cols = pl.ds(pl.multiple_of(number * 512, 512), 512)
        coeffs = jnp.dot(both, gz[:, cols], preferred_element_type=jnp.float32).astype(jnp.bfloat16)
        fitted = lax.dot_general(
            kept, coeffs, (((0,), (0,)), ((), ())), preferred_element_type=jnp.float32
        )
        out[:, cols] = (gz[0:256, cols].astype(jnp.float32) - fitted).astype(out.dtype)

    each_halo(everything, 1, lambda copy: copy.wait_send())
    for window in (0, 1):
        @pl.when(t != owners[window])
        def _():
            for stage in order:
                part_copy(stage, window, t).wait_send()
        @pl.when(t == owners[window])
        def _():
            for target in range(nta):
                if target != owners[window]:
                    basis_copy(window, target).wait_send()


def per_device(nch, nta, raw, fir_taps, start_basis):
    chans, samples = raw.shape
    taps = jnp.pad(fir_taps.astype(jnp.float32), (0, 2 * BLOCK - TAPS))[None]
    vmem = pl.BlockSpec(memory_space=pltpu.VMEM)
    return pl.pallas_call(
        functools.partial(kernel, nch, nta),
        out_shape=jax.ShapeDtypeStruct((chans, samples), jnp.bfloat16),
        in_specs=[pl.BlockSpec(memory_space=pl.ANY)] * 3,
        out_specs=vmem,
        scratch_shapes=[
            pltpu.VMEM((1, 2 * BLOCK), jnp.float32),
            pltpu.VMEM((RANK, WIN), jnp.float32),
            pltpu.SemaphoreType.DMA((2,)),
            pltpu.VMEM((672, samples + 2 * EDGE), jnp.bfloat16),
            pltpu.VMEM((640, samples), jnp.bfloat16),
            pltpu.VMEM((2 * BLOCK, BLOCK), jnp.bfloat16),
            pltpu.VMEM((14 * STRIDE, STRIDE), jnp.float32),
            pltpu.VMEM((nta, 10 * STRIDE, STRIDE), jnp.float32),
            pltpu.VMEM((WIN, WIN), jnp.bfloat16),
            pltpu.VMEM((WIN, WIN), jnp.bfloat16),
            pltpu.VMEM((2, RANK, 640), jnp.bfloat16),
            pltpu.SemaphoreType.DMA,
            pltpu.SemaphoreType.DMA((14,)),
            pltpu.SemaphoreType.DMA((14,)),
            pltpu.SemaphoreType.DMA((2, 3)),
            pltpu.SemaphoreType.DMA((nta, 3)),
            pltpu.SemaphoreType.DMA((2, nta)),
            pltpu.SemaphoreType.DMA((2,)),
        ],
        compiler_params=pltpu.CompilerParams(
            collective_id=0, has_side_effects=True, vmem_limit_bytes=60 * 1024 * 1024
        ),
    )(raw, taps, start_basis.T)


def solution(mesh):
    sizes = dict(mesh.shape)
    return jax.shard_map(
        functools.partial(per_device, sizes["ch"], sizes["ta"]),
        mesh=mesh,
        in_specs=(P("ch", "ta"), P(), P()),
        out_specs=P("ch", "ta"),
        check_vma=False,
    )
```

```python
import functools
import math

import jax
import jax.numpy as jnp
from jax import lax
from jax.experimental import pallas as pl
from jax.experimental.pallas import tpu as pltpu
from jax.sharding import PartitionSpec as P

TAPS = 129
GAUGE = 4
STRIDE = 128
RANK = 16
ITERS = 6
WIN = 512
BLOCK = 256
EDGE = 128
MESH = pl.DeviceIdType.MESH

PLACE = {2: 0, 3: 128, 1: 256, 0: 384, 4: 512}


def dot_nt(a, b):
    return lax.dot_general(a, b, (((1,), (1,)), ((), ())), preferred_element_type=jnp.float32)


def inverse_factor(gram):
    columns = [jnp.broadcast_to(gram[:, j : j + 1], (RANK, 128)) for j in range(RANK)]
    row = lax.broadcasted_iota(jnp.int32, (RANK, 128), 0)
    lane = lax.broadcasted_iota(jnp.int32, (RANK, 128), 1)
    inverse = jnp.where(row == lane % RANK, 1.0, 0.0).astype(jnp.float32)
    diagonal = jnp.ones((RANK, 128), jnp.float32)

    def spread(value, index):
        return jnp.broadcast_to(value[index : index + 1, :], (RANK, 128))

    for first in range(0, RANK, 4):
        block = range(first, first + 4)
        lead = {(i, j): spread(columns[j], i) for j in block for i in block if i >= j}
        lines = {k: spread(inverse, k) for k in block}
        scaled = {}
        for k in block:
            pivot = lead[k, k]
            diagonal = jnp.where(row == k, pivot, diagonal)
            reciprocal = 1.0 / pivot
            scaled[k] = jnp.where(row > k, columns[k] * reciprocal, 0.0)
            for j in range(k + 1, first + 4):
                ratio = lead[j, k] * reciprocal
                for i in range(j, first + 4):
                    lead[i, j] = lead[i, j] - ratio * lead[i, k]
                columns[j] = columns[j] - scaled[k] * lead[j, k]
                lines[j] = lines[j] - ratio * lines[k]
        for j in range(first + 4, RANK):
            for k in block:
                columns[j] = columns[j] - scaled[k] * spread(columns[k], j)
        for k in block:
            inverse = inverse - scaled[k] * lines[k]
    return inverse * lax.rsqrt(diagonal)


def split(value):
    high = value.astype(jnp.bfloat16)
    return high, (value - high.astype(jnp.float32)).astype(jnp.bfloat16)


def split_three(value):
    high = value.astype(jnp.bfloat16)
    rest = value - high.astype(jnp.float32)
    middle = rest.astype(jnp.bfloat16)
    return high, middle, (rest - middle.astype(jnp.float32)).astype(jnp.bfloat16)


def gram_of(parts):
    stacked = jnp.concatenate(parts, axis=0)
    terms = dot_nt(stacked, stacked)
    rows = terms[:RANK] + (terms[RANK : 2 * RANK] + terms[2 * RANK :])
    return rows[:, :RANK] + (rows[:, RANK : 2 * RANK] + rows[:, 2 * RANK :])


def apply_inverse(inverse, parts):
    lane = lax.broadcasted_iota(jnp.int32, inverse.shape, 1)
    high, middle, low = (part.astype(jnp.float32) for part in split_three(inverse))
    left = jnp.where(lane < 3 * RANK, high, jnp.where(lane < 5 * RANK, middle, low))
    left = jnp.where(lane < 6 * RANK, left, 0.0).astype(jnp.bfloat16)
    zero = jnp.zeros((2 * RANK, WIN), jnp.bfloat16)
    right = jnp.concatenate(
        [parts[0], parts[1], parts[2], parts[0], parts[1], parts[0], zero], axis=0
    )
    return jnp.dot(left, right, preferred_element_type=jnp.float32)


def kernel(
    nch, nta, raw, taps_in, start_in, out,
    taps, start, small_sem, x, gz, band, part, recv, s_hi, s_lo, basis,
    hold, top, leg_sem, top_sem,
    own_sem, halo_send, halo_recv, part_send, part_recv, basis_send, basis_recv,
):
    c = lax.axis_index("ch")
    t = lax.axis_index("ta")
    chans, samples = raw.shape
    right = EDGE + samples
    owners = (nta // 2 - 1, nta // 2)

    def exists(dc, dt):
        return (c + dc >= 0) & (c + dc < nch) & (t + dt >= 0) & (t + dt < nta)

    partners = [(dc, dt) for dc in (-1, 0, 1) for dt in (-1, 0, 1) if (dc, dt) != (0, 0)]
    partners += [(0, dt) for dt in range(1 - nta, nta) if abs(dt) > 1]

    own = pltpu.make_async_copy(raw, x.at[272:528, EDGE:right], own_sem)
    own.start()
    taps_copy = pltpu.make_async_copy(taps_in, taps, small_sem.at[0])
    start_copy = pltpu.make_async_copy(start_in, start, small_sem.at[1])
    taps_copy.start()
    start_copy.start()

    barrier = pltpu.get_barrier_semaphore()
    for dc, dt in partners:
        @pl.when(exists(dc, dt))
        def _():
            pl.semaphore_signal(barrier, inc=1, device_id=(c + dc, t + dt), device_id_type=MESH)
    near = 1 + sum(((c + dc >= 0) & (c + dc < nch)).astype(jnp.int32) for dc in (-1, 1))
    around = 1 + sum(((t + dt >= 0) & (t + dt < nta)).astype(jnp.int32) for dt in (-1, 1))
    count = near * around - 1 + nta - around
    if nch == 8:
        turning = (c % 4 == 0) | (c % 4 == 3)
        @pl.when(turning)
        def _():
            for other in ((c + 4) % 8, jnp.where(c < 4, 3 - c, 11 - c)):
                pl.semaphore_signal(barrier, inc=1, device_id=(other, t), device_id_type=MESH)
        count = count + jnp.where(turning, 2, 0)
    pl.semaphore_wait(barrier, count)

    mid = (EDGE, right)
    whole = (0, samples)
    low, high = (0, EDGE), (right, right + EDGE)
    head, tail = (0, EDGE), (samples - EDGE, samples)
    kinds = [
        (0, 1, (0, 256), tail, (272, 528), low),
        (0, -1, (0, 256), head, (272, 528), high),
        (1, 0, (240, 256), whole, (256, 272), mid),
        (-1, 0, (0, 16), whole, (528, 544), mid),
        (1, 1, (0, 256), tail, (16, 272), low),
        (1, -1, (0, 256), head, (16, 272), high),
        (-1, 1, (0, 144), tail, (528, 672), low),
        (-1, -1, (0, 144), head, (528, 672), high),
        (1, 0, (112, 240), whole, (128, 256), mid),
        (-1, 0, (16, 80), whole, (544, 608), mid),
        (-1, 0, (80, 144), whole, (608, 672), mid),
        (1, 0, (0, 112), whole, (16, 128), mid),
    ]
    detours = [(11, 3, 7, 4), (10, 4, 0, 3)] if nch == 8 else []

    def halo(index):
        dc, dt, rows, cols, to_rows, to_cols = kinds[index]
        return pltpu.make_async_remote_copy(
            src_ref=raw.at[rows[0] : rows[1], cols[0] : cols[1]],
            dst_ref=x.at[to_rows[0] : to_rows[1], to_cols[0] : to_cols[1]],
            send_sem=halo_send.at[index],
            recv_sem=halo_recv.at[index],
            device_id=(c + dc, t + dt),
            device_id_type=MESH,
        )

    def first_leg(index, by):
        rows = kinds[index][2]
        return pltpu.make_async_remote_copy(
            src_ref=raw.at[rows[0] : rows[1]],
            dst_ref=hold.at[0 : rows[1] - rows[0]],
            send_sem=leg_sem.at[0],
            recv_sem=leg_sem.at[1],
            device_id=(by, t),
            device_id_type=MESH,
        )

    def second_leg(index, to):
        rows, _, to_rows, to_cols = kinds[index][2:]
        return pltpu.make_async_remote_copy(
            src_ref=hold.at[0 : rows[1] - rows[0]],
            dst_ref=x.at[to_rows[0] : to_rows[1], to_cols[0] : to_cols[1]],
            send_sem=leg_sem.at[2],
            recv_sem=halo_recv.at[index],
            device_id=(to, t),
            device_id_type=MESH,
        )

    def each_halo(indices, sign, act):
        for index in indices:
            dc, dt = kinds[index][:2]
            wanted = exists(sign * dc, sign * dt)
            if sign > 0:
                for number, source, _, _ in detours:
                    if number == index:
                        wanted = wanted & (c != source)
            @pl.when(wanted)
            def _():
                act(halo(index))

    everything = range(len(kinds))
    each_halo(range(0, 8), 1, lambda copy: copy.start())
    for index, source, by, _ in detours:
        @pl.when(c == source)
        def _():
            first_leg(index, by).start()
    each_halo(range(8, 12), 1, lambda copy: copy.start())

    @pl.when(t == 0)
    def _():
        x[16:672, 0:EDGE] = jnp.zeros((656, EDGE), x.dtype)

    @pl.when(t == nta - 1)
    def _():
        x[16:672, right : right + EDGE] = jnp.zeros((656, EDGE), x.dtype)

    @pl.when(c == 0)
    def _():
        x[256:272, :] = jnp.zeros((16, x.shape[1]), x.dtype)

    x[0:16, :] = jnp.zeros((16, x.shape[1]), x.dtype)

    @pl.when(c == nch - 1)
    def _():
        x[528:544, :] = jnp.zeros((16, x.shape[1]), x.dtype)
        gz[512:640, :] = jnp.zeros((STRIDE, samples), gz.dtype)

    @pl.when(c == 0)
    def _():
        gz[256:512, :] = jnp.zeros((2 * STRIDE, samples), gz.dtype)

    taps_copy.wait()
    start_copy.wait()
    lines = jnp.broadcast_to(taps[...], (BLOCK, 2 * BLOCK))
    lines = pltpu.roll(lines, 64, 1, stride=1, stride_axis=0)
    band[...] = lines.T.astype(band.dtype)

    @pl.when(t == 0)
    def _():
        x[:, 0:EDGE] = jnp.zeros((x.shape[0], EDGE), x.dtype)

    @pl.when(t == nta - 1)
    def _():
        x[:, right : right + EDGE] = jnp.zeros((x.shape[0], EDGE), x.dtype)

    @pl.when(c == 0)
    def _():
        x[256:272, :] = jnp.zeros((16, x.shape[1]), x.dtype)

    @pl.when(c == 1)
    def _():
        x[0:16, :] = jnp.zeros((16, x.shape[1]), x.dtype)

    @pl.when(c == nch - 1)
    def _():
        x[528:544, :] = jnp.zeros((16, x.shape[1]), x.dtype)
        gz[512:640, :] = jnp.zeros((STRIDE, samples), gz.dtype)

    @pl.when(c == 0)
    def _():
        gz[256:512, :] = jnp.zeros((2 * STRIDE, samples), gz.dtype)

    def gauge(first, count):
        rows = STRIDE * count + 32
        together = math.gcd(samples // BLOCK, 5)
        @pl.loop(0, samples // (BLOCK * together))
        def _(number):
            start_col = pl.multiple_of(number * (BLOCK * together), BLOCK)
            pieces = [
                x[STRIDE * first : STRIDE * first + rows, pl.ds(start_col + BLOCK * p, 2 * BLOCK)]
                for p in range(together)
            ]
            filtered = jnp.dot(
                jnp.concatenate(pieces, axis=0), band[...], preferred_element_type=jnp.float32
            )
            for p in range(together):
                for step in range(count):
                    base = rows * p + STRIDE * step
                    upper = filtered[base + 20 : base + 20 + STRIDE]
                    lower = filtered[base + 12 : base + 12 + STRIDE]
                    place = PLACE[first + step]
                    gz[place : place + STRIDE, pl.ds(start_col + BLOCK * p, BLOCK)] = (
                        upper - lower
                    ).astype(gz.dtype)

    def products(groups):
        chunk = 1024
        for left, right_tile, place in groups:
            part[place : place + left[1] - left[0], :] = jnp.zeros((left[1] - left[0], STRIDE), jnp.float32)
        @pl.loop(0, samples // chunk)
        def _(number):
            cols = pl.ds(pl.multiple_of(number * chunk, chunk), chunk)
            for left, right_tile, place in groups:
                part[place : place + left[1] - left[0], :] += dot_nt(
                    gz[left[0] : left[1], cols], gz[right_tile : right_tile + STRIDE, cols]
                )

    spans = {
        ("own", 0): (0, 384, 0), ("own", 1): (0, 384, 0),
        ("next", 0): (384, 768, 384), ("next", 1): (384, 768, 384),
        ("far", 0): (1280, 1792, 768), ("far", 1): (768, 1280, 768),
    }
    order = {"own": 0, "next": 1, "far": 2}

    def part_copy(stage, window, source):
        begin, end, land = spans[stage, window]
        return pltpu.make_async_remote_copy(
            src_ref=part.at[begin:end],
            dst_ref=recv.at[source, land : land + end - begin],
            send_sem=part_send.at[window, order[stage]],
            recv_sem=part_recv.at[source, order[stage]],
            device_id=(c, owners[window]),
            device_id_type=MESH,
        )

    def send_part(stage, window):
        @pl.when(t != owners[window])
        def _():
            part_copy(stage, window, t).start()

    own.wait()
    each_halo(range(0, 8), -1, lambda copy: copy.wait_recv())
    gauge(2, 2)
    top_copy = pltpu.make_async_remote_copy(
        src_ref=gz.at[0:16],
        dst_ref=top,
        send_sem=top_sem.at[0],
        recv_sem=top_sem.at[1],
        device_id=(c + 1, t),
        device_id_type=MESH,
    )
    @pl.when(c < nch - 1)
    def _():
        top_copy.start()
    products([((0, 256), 0, 0), ((128, 256), 128, 256)])
    send_part("own", 0)
    send_part("own", 1)

    each_halo([8], -1, lambda copy: copy.wait_recv())
    @pl.when(c > 0)
    def _():
        gauge(1, 1)
    products([((0, 384), 256, 384)])
    send_part("next", 0)
    send_part("next", 1)

    def tile_after():
        each_halo([9, 10], -1, lambda copy: copy.wait_recv())
        @pl.when(c < nch - 1)
        def _():
            gauge(4, 1)
        products([((0, 384), 512, 768), ((512, 640), 512, 1152)])
        send_part("far", 1)

    def first_tile():
        each_halo([11], -1, lambda copy: copy.wait_recv())
        @pl.when(c > 0)
        def _():
            gauge(0, 1)
            top_copy.wait_recv()
            gz[384:400, :] = top[...]
        products([((0, 512), 384, 1280)])
        send_part("far", 0)

    for index, _, by, to in detours:
        @pl.when(c == by)
        def _():
            first_leg(index, by).wait_recv()
            second_leg(index, to).start()

    @pl.when(c % 2 == 1)
    def _():
        first_tile()
    tile_after()
    @pl.when(c % 2 == 0)
    def _():
        first_tile()

    total_time = samples * nta

    def solve(window):
        for source in range(nta):
            if source != owners[window]:
                for stage in order:
                    part_copy(stage, window, source).wait_recv()

        blocks = {
            (0, 0): ("own", 0), (1, 0): ("own", 1), (1, 1): ("own", 2),
            (0, 2): ("next", 0), (1, 2): ("next", 1), (2, 2): ("next", 2),
            (0, 3): ("far", 0), (1, 3): ("far", 1), (2, 3): ("far", 2), (3, 3): ("far", 3),
        }
        for (p, q), (stage, number) in blocks.items():
            begin, _, land = spans[stage, window]
            begin, land = begin + STRIDE * number, land + STRIDE * number
            value = part[begin : begin + STRIDE, :]
            for source in range(nta):
                if source != owners[window]:
                    value = value + recv[source, land : land + STRIDE, :]
            value = value * (1.0 / total_time)
            for row, col, block in ((p, q, value), (q, p, value.T)):
                if (row, col) == (p, q) or p != q:
                    high_part, low_part = split(block)
                    where = (slice(STRIDE * row, STRIDE * (row + 1)), slice(STRIDE * col, STRIDE * (col + 1)))
                    s_hi[where] = high_part
                    s_lo[where] = low_part

        def sweep(_, current):
            high_part, low_part = split(current)
            both = jnp.concatenate([high_part, low_part], axis=0)
            image = jnp.dot(both, s_hi[...], preferred_element_type=jnp.float32)
            image = image[:RANK] + image[RANK:] + jnp.dot(
                high_part, s_lo[...], preferred_element_type=jnp.float32
            )
            parts = split_three(image)
            return apply_inverse(inverse_factor(gram_of(parts)), parts)

        places = (2, 3, 1, 0) if window == 0 else (1, 2, 0, 3)
        first = jnp.concatenate([start[:, STRIDE * p : STRIDE * (p + 1)] for p in places], axis=1)
        found = lax.fori_loop(0, ITERS, sweep, first).astype(jnp.bfloat16)
        zero = jnp.zeros((RANK, STRIDE), jnp.bfloat16)
        last = [found[:, 384:512], zero] if window == 0 else [zero, found[:, 384:512]]
        basis[window] = jnp.concatenate([found[:, :384]] + last, axis=1)

    def basis_copy(window, target):
        return pltpu.make_async_remote_copy(
            src_ref=basis.at[window],
            dst_ref=basis.at[window],
            send_sem=basis_send.at[window, target],
            recv_sem=basis_recv.at[window],
            device_id=(c, target),
            device_id_type=MESH,
        )

    for window in (0, 1):
        @pl.when(t == owners[window])
        def _():
            solve(window)
            for target in range(nta):
                if target != owners[window]:
                    basis_copy(window, target).start()

    for window in (0, 1):
        @pl.when(t != owners[window])
        def _():
            basis_copy(window, owners[window]).wait_recv()

    both = jnp.concatenate([basis[0], basis[1]], axis=0)
    nothing = jnp.zeros((RANK, STRIDE), jnp.bfloat16)
    kept = jnp.concatenate(
        [
            jnp.concatenate([basis[0][:, 0:128], nothing], axis=1),
            jnp.concatenate([nothing, basis[1][:, 128:256]], axis=1),
        ],
        axis=0,
    )

    @pl.loop(0, samples // 512)
    def _(number):
        cols = pl.ds(pl.multiple_of(number * 512, 512), 512)
        coeffs = jnp.dot(both, gz[:, cols], preferred_element_type=jnp.float32).astype(jnp.bfloat16)
        fitted = lax.dot_general(
            kept, coeffs, (((0,), (0,)), ((), ())), preferred_element_type=jnp.float32
        )
        out[:, cols] = (gz[0:256, cols].astype(jnp.float32) - fitted).astype(out.dtype)

    each_halo(everything, 1, lambda copy: copy.wait_send())
    @pl.when(c < nch - 1)
    def _():
        top_copy.wait_send()
    for index, source, by, to in detours:
        @pl.when(c == source)
        def _():
            first_leg(index, by).wait_send()
        @pl.when(c == by)
        def _():
            second_leg(index, to).wait_send()
    for window in (0, 1):
        @pl.when(t != owners[window])
        def _():
            for stage in order:
                part_copy(stage, window, t).wait_send()
        @pl.when(t == owners[window])
        def _():
            for target in range(nta):
                if target != owners[window]:
                    basis_copy(window, target).wait_send()


def per_device(nch, nta, raw, fir_taps, start_basis):
    chans, samples = raw.shape
    taps = jnp.pad(fir_taps.astype(jnp.float32), (0, 2 * BLOCK - TAPS))[None]
    vmem = pl.BlockSpec(memory_space=pltpu.VMEM)
    return pl.pallas_call(
        functools.partial(kernel, nch, nta),
        out_shape=jax.ShapeDtypeStruct((chans, samples), jnp.bfloat16),
        in_specs=[pl.BlockSpec(memory_space=pl.ANY)] * 3,
        out_specs=vmem,
        scratch_shapes=[
            pltpu.VMEM((1, 2 * BLOCK), jnp.float32),
            pltpu.VMEM((RANK, WIN), jnp.float32),
            pltpu.SemaphoreType.DMA((2,)),
            pltpu.VMEM((672, samples + 2 * EDGE), jnp.bfloat16),
            pltpu.VMEM((640, samples), jnp.bfloat16),
            pltpu.VMEM((2 * BLOCK, BLOCK), jnp.bfloat16),
            pltpu.VMEM((14 * STRIDE, STRIDE), jnp.float32),
            pltpu.VMEM((nta, 10 * STRIDE, STRIDE), jnp.float32),
            pltpu.VMEM((WIN, WIN), jnp.bfloat16),
            pltpu.VMEM((WIN, WIN), jnp.bfloat16),
            pltpu.VMEM((2, RANK, 640), jnp.bfloat16),
            pltpu.VMEM((112, samples), jnp.bfloat16),
            pltpu.VMEM((16, samples), jnp.bfloat16),
            pltpu.SemaphoreType.DMA((3,)),
            pltpu.SemaphoreType.DMA((2,)),
            pltpu.SemaphoreType.DMA,
            pltpu.SemaphoreType.DMA((12,)),
            pltpu.SemaphoreType.DMA((12,)),
            pltpu.SemaphoreType.DMA((2, 3)),
            pltpu.SemaphoreType.DMA((nta, 3)),
            pltpu.SemaphoreType.DMA((2, nta)),
            pltpu.SemaphoreType.DMA((2,)),
        ],
        compiler_params=pltpu.CompilerParams(
            collective_id=0, has_side_effects=True, vmem_limit_bytes=60 * 1024 * 1024
        ),
    )(raw, taps, start_basis.T)


def solution(mesh):
    sizes = dict(mesh.shape)
    return jax.shard_map(
        functools.partial(per_device, sizes["ch"], sizes["ta"]),
        mesh=mesh,
        in_specs=(P("ch", "ta"), P(), P()),
        out_specs=P("ch", "ta"),
        check_vma=False,
    )
```

```python
import functools
import math

import jax
import jax.numpy as jnp
from jax import lax
from jax.experimental import pallas as pl
from jax.experimental.pallas import tpu as pltpu
from jax.sharding import PartitionSpec as P

TAPS = 129
GAUGE = 4
STRIDE = 128
RANK = 16
ITERS = 6
WIN = 512
BLOCK = 256
EDGE = 128
MESH = pl.DeviceIdType.MESH

PLACE = {2: 0, 3: 128, 1: 256, 0: 384, 4: 512}


def dot_nt(a, b):
    return lax.dot_general(a, b, (((1,), (1,)), ((), ())), preferred_element_type=jnp.float32)


def inverse_factor(gram):
    columns = [jnp.broadcast_to(gram[:, j : j + 1], (RANK, 128)) for j in range(RANK)]
    row = lax.broadcasted_iota(jnp.int32, (RANK, 128), 0)
    lane = lax.broadcasted_iota(jnp.int32, (RANK, 128), 1)
    inverse = jnp.where(row == lane % RANK, 1.0, 0.0).astype(jnp.float32)
    diagonal = jnp.ones((RANK, 128), jnp.float32)

    def spread(value, index):
        return jnp.broadcast_to(value[index : index + 1, :], (RANK, 128))

    for first in range(0, RANK, 4):
        block = range(first, first + 4)
        lead = {(i, j): spread(columns[j], i) for j in block for i in block if i >= j}
        lines = {k: spread(inverse, k) for k in block}
        scaled = {}
        for k in block:
            pivot = lead[k, k]
            diagonal = jnp.where(row == k, pivot, diagonal)
            reciprocal = 1.0 / pivot
            scaled[k] = jnp.where(row > k, columns[k] * reciprocal, 0.0)
            for j in range(k + 1, first + 4):
                ratio = lead[j, k] * reciprocal
                for i in range(j, first + 4):
                    lead[i, j] = lead[i, j] - ratio * lead[i, k]
                columns[j] = columns[j] - scaled[k] * lead[j, k]
                lines[j] = lines[j] - ratio * lines[k]
        for j in range(first + 4, RANK):
            for k in block:
                columns[j] = columns[j] - scaled[k] * spread(columns[k], j)
        for k in block:
            inverse = inverse - scaled[k] * lines[k]
    return inverse * lax.rsqrt(diagonal)


def split(value):
    high = value.astype(jnp.bfloat16)
    return high, (value - high.astype(jnp.float32)).astype(jnp.bfloat16)


def split_three(value):
    high = value.astype(jnp.bfloat16)
    rest = value - high.astype(jnp.float32)
    middle = rest.astype(jnp.bfloat16)
    return high, middle, (rest - middle.astype(jnp.float32)).astype(jnp.bfloat16)


def gram_of(parts):
    stacked = jnp.concatenate(parts, axis=0)
    terms = dot_nt(stacked, stacked)
    rows = terms[:RANK] + (terms[RANK : 2 * RANK] + terms[2 * RANK :])
    return rows[:, :RANK] + (rows[:, RANK : 2 * RANK] + rows[:, 2 * RANK :])


def apply_inverse(inverse, parts):
    lane = lax.broadcasted_iota(jnp.int32, inverse.shape, 1)
    high, middle, low = (part.astype(jnp.float32) for part in split_three(inverse))
    left = jnp.where(lane < 3 * RANK, high, jnp.where(lane < 5 * RANK, middle, low))
    left = jnp.where(lane < 6 * RANK, left, 0.0).astype(jnp.bfloat16)
    zero = jnp.zeros((2 * RANK, WIN), jnp.bfloat16)
    right = jnp.concatenate(
        [parts[0], parts[1], parts[2], parts[0], parts[1], parts[0], zero], axis=0
    )
    return jnp.dot(left, right, preferred_element_type=jnp.float32)


def kernel(
    nch, nta, raw, taps_in, start_in, out,
    taps, start, small_sem, x, gz, band, part, recv, s_hi, s_lo, basis,
    hold, top, leg_sem, top_sem,
    own_sem, halo_send, halo_recv, part_send, part_recv, basis_send, basis_recv,
):
    c = lax.axis_index("ch")
    t = lax.axis_index("ta")
    chans, samples = raw.shape
    right = EDGE + samples
    owners = (nta // 2 - 1, nta // 2)

    def exists(dc, dt):
        return (c + dc >= 0) & (c + dc < nch) & (t + dt >= 0) & (t + dt < nta)

    partners = [(dc, dt) for dc in (-1, 0, 1) for dt in (-1, 0, 1) if (dc, dt) != (0, 0)]
    partners += [(0, dt) for dt in range(1 - nta, nta) if abs(dt) > 1]

    own = pltpu.make_async_copy(raw, x.at[272:528, EDGE:right], own_sem)
    own.start()
    taps_copy = pltpu.make_async_copy(taps_in, taps, small_sem.at[0])
    start_copy = pltpu.make_async_copy(start_in, start, small_sem.at[1])
    taps_copy.start()
    start_copy.start()

    barrier = pltpu.get_barrier_semaphore()
    for dc, dt in partners:
        @pl.when(exists(dc, dt))
        def _():
            pl.semaphore_signal(barrier, inc=1, device_id=(c + dc, t + dt), device_id_type=MESH)
    near = 1 + sum(((c + dc >= 0) & (c + dc < nch)).astype(jnp.int32) for dc in (-1, 1))
    around = 1 + sum(((t + dt >= 0) & (t + dt < nta)).astype(jnp.int32) for dt in (-1, 1))
    count = near * around - 1 + nta - around
    if nch == 8:
        turning = (c % 4 == 0) | (c % 4 == 3)
        @pl.when(turning)
        def _():
            for other in ((c + 4) % 8, jnp.where(c < 4, 3 - c, 11 - c)):
                pl.semaphore_signal(barrier, inc=1, device_id=(other, t), device_id_type=MESH)
        count = count + jnp.where(turning, 2, 0)
    pl.semaphore_wait(barrier, count)

    mid = (EDGE, right)
    whole = (0, samples)
    low, high = (0, EDGE), (right, right + EDGE)
    head, tail = (0, EDGE), (samples - EDGE, samples)
    kinds = [
        (0, 1, (0, 256), tail, (272, 528), low),
        (0, -1, (0, 256), head, (272, 528), high),
        (1, 0, (240, 256), whole, (256, 272), mid),
        (-1, 0, (0, 16), whole, (528, 544), mid),
        (1, 1, (0, 256), tail, (16, 272), low),
        (1, -1, (0, 256), head, (16, 272), high),
        (-1, 1, (0, 144), tail, (528, 672), low),
        (-1, -1, (0, 144), head, (528, 672), high),
        (1, 0, (112, 240), whole, (128, 256), mid),
        (-1, 0, (16, 80), whole, (544, 608), mid),
        (-1, 0, (80, 144), whole, (608, 672), mid),
        (1, 0, (0, 112), whole, (16, 128), mid),
    ]
    detours = [(11, 3, 7, 4), (10, 4, 0, 3)] if nch == 8 else []

    def halo(index):
        dc, dt, rows, cols, to_rows, to_cols = kinds[index]
        return pltpu.make_async_remote_copy(
            src_ref=raw.at[rows[0] : rows[1], cols[0] : cols[1]],
            dst_ref=x.at[to_rows[0] : to_rows[1], to_cols[0] : to_cols[1]],
            send_sem=halo_send.at[index],
            recv_sem=halo_recv.at[index],
            device_id=(c + dc, t + dt),
            device_id_type=MESH,
        )

    def first_leg(index, by):
        rows = kinds[index][2]
        return pltpu.make_async_remote_copy(
            src_ref=raw.at[rows[0] : rows[1]],
            dst_ref=hold.at[0 : rows[1] - rows[0]],
            send_sem=leg_sem.at[0],
            recv_sem=leg_sem.at[1],
            device_id=(by, t),
            device_id_type=MESH,
        )

    def second_leg(index, to):
        rows, _, to_rows, to_cols = kinds[index][2:]
        return pltpu.make_async_remote_copy(
            src_ref=hold.at[0 : rows[1] - rows[0]],
            dst_ref=x.at[to_rows[0] : to_rows[1], to_cols[0] : to_cols[1]],
            send_sem=leg_sem.at[2],
            recv_sem=halo_recv.at[index],
            device_id=(to, t),
            device_id_type=MESH,
        )

    def each_halo(indices, sign, act):
        for index in indices:
            dc, dt = kinds[index][:2]
            wanted = exists(sign * dc, sign * dt)
            if sign > 0:
                for number, source, _, _ in detours:
                    if number == index:
                        wanted = wanted & (c != source)
            @pl.when(wanted)
            def _():
                act(halo(index))

    everything = range(len(kinds))
    each_halo(range(0, 8), 1, lambda copy: copy.start())
    for index, source, by, _ in detours:
        @pl.when(c == source)
        def _():
            first_leg(index, by).start()
    each_halo(range(8, 12), 1, lambda copy: copy.start())

    @pl.when(t == 0)
    def _():
        x[16:672, 0:EDGE] = jnp.zeros((656, EDGE), x.dtype)

    @pl.when(t == nta - 1)
    def _():
        x[16:672, right : right + EDGE] = jnp.zeros((656, EDGE), x.dtype)

    @pl.when(c == 0)
    def _():
        x[256:272, :] = jnp.zeros((16, x.shape[1]), x.dtype)

    x[0:16, :] = jnp.zeros((16, x.shape[1]), x.dtype)

    @pl.when(c == nch - 1)
    def _():
        x[528:544, :] = jnp.zeros((16, x.shape[1]), x.dtype)
        gz[512:640, :] = jnp.zeros((STRIDE, samples), gz.dtype)

    @pl.when(c == 0)
    def _():
        gz[256:512, :] = jnp.zeros((2 * STRIDE, samples), gz.dtype)

    taps_copy.wait()
    start_copy.wait()
    lines = jnp.broadcast_to(taps[...], (BLOCK, 2 * BLOCK))
    lines = pltpu.roll(lines, 64, 1, stride=1, stride_axis=0)
    band[...] = lines.T.astype(band.dtype)

    @pl.when(t == 0)
    def _():
        x[:, 0:EDGE] = jnp.zeros((x.shape[0], EDGE), x.dtype)

    @pl.when(t == nta - 1)
    def _():
        x[:, right : right + EDGE] = jnp.zeros((x.shape[0], EDGE), x.dtype)

    @pl.when(c == 0)
    def _():
        x[256:272, :] = jnp.zeros((16, x.shape[1]), x.dtype)

    @pl.when(c == 1)
    def _():
        x[0:16, :] = jnp.zeros((16, x.shape[1]), x.dtype)

    @pl.when(c == nch - 1)
    def _():
        x[528:544, :] = jnp.zeros((16, x.shape[1]), x.dtype)
        gz[512:640, :] = jnp.zeros((STRIDE, samples), gz.dtype)

    @pl.when(c == 0)
    def _():
        gz[256:512, :] = jnp.zeros((2 * STRIDE, samples), gz.dtype)

    def gauge(first, count):
        rows = STRIDE * count + 32
        together = math.gcd(samples // BLOCK, 5)
        @pl.loop(0, samples // (BLOCK * together))
        def _(number):
            start_col = pl.multiple_of(number * (BLOCK * together), BLOCK)
            pieces = [
                x[STRIDE * first : STRIDE * first + rows, pl.ds(start_col + BLOCK * p, 2 * BLOCK)]
                for p in range(together)
            ]
            filtered = jnp.dot(
                jnp.concatenate(pieces, axis=0), band[...], preferred_element_type=jnp.float32
            )
            for p in range(together):
                for step in range(count):
                    base = rows * p + STRIDE * step
                    upper = filtered[base + 20 : base + 20 + STRIDE]
                    lower = filtered[base + 12 : base + 12 + STRIDE]
                    place = PLACE[first + step]
                    gz[place : place + STRIDE, pl.ds(start_col + BLOCK * p, BLOCK)] = (
                        upper - lower
                    ).astype(gz.dtype)

    def products(groups):
        chunk = 1024
        for left, right_tile, place in groups:
            part[place : place + left[1] - left[0], :] = jnp.zeros((left[1] - left[0], STRIDE), jnp.float32)
        @pl.loop(0, samples // chunk)
        def _(number):
            cols = pl.ds(pl.multiple_of(number * chunk, chunk), chunk)
            for left, right_tile, place in groups:
                part[place : place + left[1] - left[0], :] += dot_nt(
                    gz[left[0] : left[1], cols], gz[right_tile : right_tile + STRIDE, cols]
                )

    spans = {
        ("own", 0): (0, 384, 0), ("own", 1): (0, 384, 0),
        ("next", 0): (384, 768, 384), ("next", 1): (384, 768, 384),
        ("far", 0): (1280, 1792, 768), ("far", 1): (768, 1280, 768),
    }
    order = {"own": 0, "next": 1, "far": 2}

    def part_copy(stage, window, source):
        begin, end, land = spans[stage, window]
        return pltpu.make_async_remote_copy(
            src_ref=part.at[begin:end],
            dst_ref=recv.at[source, land : land + end - begin],
            send_sem=part_send.at[window, order[stage]],
            recv_sem=part_recv.at[source, order[stage]],
            device_id=(c, owners[window]),
            device_id_type=MESH,
        )

    def send_part(stage, window):
        @pl.when(t != owners[window])
        def _():
            part_copy(stage, window, t).start()

    own.wait()
    each_halo(range(0, 8), -1, lambda copy: copy.wait_recv())
    gauge(2, 2)
    top_copy = pltpu.make_async_remote_copy(
        src_ref=gz.at[0:16],
        dst_ref=top,
        send_sem=top_sem.at[0],
        recv_sem=top_sem.at[1],
        device_id=(c + 1, t),
        device_id_type=MESH,
    )
    @pl.when(c < nch - 1)
    def _():
        top_copy.start()
    products([((0, 256), 0, 0), ((128, 256), 128, 256)])
    send_part("own", 0)
    send_part("own", 1)

    each_halo([8], -1, lambda copy: copy.wait_recv())
    @pl.when(c > 0)
    def _():
        gauge(1, 1)
    products([((0, 384), 256, 384)])
    send_part("next", 0)
    send_part("next", 1)

    def tile_after():
        each_halo([9, 10], -1, lambda copy: copy.wait_recv())
        @pl.when(c < nch - 1)
        def _():
            gauge(4, 1)
        products([((0, 384), 512, 768), ((512, 640), 512, 1152)])
        send_part("far", 1)

    def first_tile():
        each_halo([11], -1, lambda copy: copy.wait_recv())
        @pl.when(c > 0)
        def _():
            gauge(0, 1)
            top_copy.wait_recv()
            gz[384:400, :] = top[...]
        products([((0, 512), 384, 1280)])
        send_part("far", 0)

    for index, _, by, to in detours:
        @pl.when(c == by)
        def _():
            first_leg(index, by).wait_recv()
            second_leg(index, to).start()

    @pl.when(c % 2 == 1)
    def _():
        first_tile()
    tile_after()
    @pl.when(c % 2 == 0)
    def _():
        first_tile()

    total_time = samples * nta

    def solve(window):
        for source in range(nta):
            if source != owners[window]:
                for stage in order:
                    part_copy(stage, window, source).wait_recv()

        blocks = {
            (0, 0): ("own", 0), (1, 0): ("own", 1), (1, 1): ("own", 2),
            (0, 2): ("next", 0), (1, 2): ("next", 1), (2, 2): ("next", 2),
            (0, 3): ("far", 0), (1, 3): ("far", 1), (2, 3): ("far", 2), (3, 3): ("far", 3),
        }
        for (p, q), (stage, number) in blocks.items():
            begin, _, land = spans[stage, window]
            begin, land = begin + STRIDE * number, land + STRIDE * number
            value = part[begin : begin + STRIDE, :]
            for source in range(nta):
                if source != owners[window]:
                    value = value + recv[source, land : land + STRIDE, :]
            value = value * (1.0 / total_time)
            for row, col, block in ((p, q, value), (q, p, value.T)):
                if (row, col) == (p, q) or p != q:
                    high_part, low_part = split(block)
                    where = (slice(STRIDE * row, STRIDE * (row + 1)), slice(STRIDE * col, STRIDE * (col + 1)))
                    s_hi[where] = high_part
                    s_lo[where] = low_part

        def sweep(_, current):
            high_part, low_part = split(current)
            both = jnp.concatenate([high_part, low_part], axis=0)
            image = jnp.dot(both, s_hi[...], preferred_element_type=jnp.float32)
            image = image[:RANK] + image[RANK:] + jnp.dot(
                high_part, s_lo[...], preferred_element_type=jnp.float32
            )
            parts = split_three(image)
            return apply_inverse(inverse_factor(gram_of(parts)), parts)

        places = (2, 3, 1, 0) if window == 0 else (1, 2, 0, 3)
        first = jnp.concatenate([start[:, STRIDE * p : STRIDE * (p + 1)] for p in places], axis=1)
        found = lax.fori_loop(0, ITERS, sweep, first).astype(jnp.bfloat16)
        zero = jnp.zeros((RANK, STRIDE), jnp.bfloat16)
        last = [found[:, 384:512], zero] if window == 0 else [zero, found[:, 384:512]]
        basis[window] = jnp.concatenate([found[:, :384]] + last, axis=1)

    def basis_copy(window, target):
        return pltpu.make_async_remote_copy(
            src_ref=basis.at[window],
            dst_ref=basis.at[window],
            send_sem=basis_send.at[window, target],
            recv_sem=basis_recv.at[window],
            device_id=(c, target),
            device_id_type=MESH,
        )

    for window in (0, 1):
        @pl.when(t == owners[window])
        def _():
            solve(window)
            for target in range(nta):
                if target != owners[window]:
                    basis_copy(window, target).start()

    for window in (0, 1):
        @pl.when(t != owners[window])
        def _():
            basis_copy(window, owners[window]).wait_recv()

    both = jnp.concatenate([basis[0], basis[1]], axis=0)
    nothing = jnp.zeros((RANK, STRIDE), jnp.bfloat16)
    kept = jnp.concatenate(
        [
            jnp.concatenate([basis[0][:, 0:128], nothing], axis=1),
            jnp.concatenate([nothing, basis[1][:, 128:256]], axis=1),
        ],
        axis=0,
    )

    @pl.loop(0, samples // 512)
    def _(number):
        cols = pl.ds(pl.multiple_of(number * 512, 512), 512)
        coeffs = jnp.dot(both, gz[:, cols], preferred_element_type=jnp.float32).astype(jnp.bfloat16)
        fitted = lax.dot_general(
            kept, coeffs, (((0,), (0,)), ((), ())), preferred_element_type=jnp.float32
        )
        out[:, cols] = (gz[0:256, cols].astype(jnp.float32) - fitted).astype(out.dtype)

    each_halo(everything, 1, lambda copy: copy.wait_send())
    @pl.when(c < nch - 1)
    def _():
        top_copy.wait_send()
    for index, source, by, to in detours:
        @pl.when(c == source)
        def _():
            first_leg(index, by).wait_send()
        @pl.when(c == by)
        def _():
            second_leg(index, to).wait_send()
    for window in (0, 1):
        @pl.when(t != owners[window])
        def _():
            for stage in order:
                part_copy(stage, window, t).wait_send()
        @pl.when(t == owners[window])
        def _():
            for target in range(nta):
                if target != owners[window]:
                    basis_copy(window, target).wait_send()


def per_device(nch, nta, raw, fir_taps, start_basis):
    chans, samples = raw.shape
    taps = jnp.pad(fir_taps.astype(jnp.float32), (0, 2 * BLOCK - TAPS))[None]
    vmem = pl.BlockSpec(memory_space=pltpu.VMEM)
    return pl.pallas_call(
        functools.partial(kernel, nch, nta),
        out_shape=jax.ShapeDtypeStruct((chans, samples), jnp.bfloat16),
        in_specs=[pl.BlockSpec(memory_space=pl.ANY)] * 3,
        out_specs=vmem,
        scratch_shapes=[
            pltpu.VMEM((1, 2 * BLOCK), jnp.float32),
            pltpu.VMEM((RANK, WIN), jnp.float32),
            pltpu.SemaphoreType.DMA((2,)),
            pltpu.VMEM((672, samples + 2 * EDGE), jnp.bfloat16),
            pltpu.VMEM((640, samples), jnp.bfloat16),
            pltpu.VMEM((2 * BLOCK, BLOCK), jnp.bfloat16),
            pltpu.VMEM((14 * STRIDE, STRIDE), jnp.float32),
            pltpu.VMEM((nta, 10 * STRIDE, STRIDE), jnp.float32),
            pltpu.VMEM((WIN, WIN), jnp.bfloat16),
            pltpu.VMEM((WIN, WIN), jnp.bfloat16),
            pltpu.VMEM((2, RANK, 640), jnp.bfloat16),
            pltpu.VMEM((112, samples), jnp.bfloat16),
            pltpu.VMEM((16, samples), jnp.bfloat16),
            pltpu.SemaphoreType.DMA((3,)),
            pltpu.SemaphoreType.DMA((2,)),
            pltpu.SemaphoreType.DMA,
            pltpu.SemaphoreType.DMA((12,)),
            pltpu.SemaphoreType.DMA((12,)),
            pltpu.SemaphoreType.DMA((2, 3)),
            pltpu.SemaphoreType.DMA((nta, 3)),
            pltpu.SemaphoreType.DMA((2, nta)),
            pltpu.SemaphoreType.DMA((2,)),
        ],
        compiler_params=pltpu.CompilerParams(
            collective_id=0, has_side_effects=True, vmem_limit_bytes=50 * 1024 * 1024
        ),
    )(raw, taps, start_basis.T)


def solution(mesh):
    sizes = dict(mesh.shape)
    return jax.shard_map(
        functools.partial(per_device, sizes["ch"], sizes["ta"]),
        mesh=mesh,
        in_specs=(P("ch", "ta"), P(), P()),
        out_specs=P("ch", "ta"),
        check_vma=False,
    )
```
